32 devices in a mesh: clus: 8 (over y, x, core), dir: 4 (over z).
Axes of the slice: x: 2, y: 2, z: 4, core: 2. Of those that a mesh axis runs over, the one named last changes fastest.
Arguments:
- sources: bfloat16 [96, 32768], P(None, ('clus', 'dir')), may hold values from -6 to 6
- live_counts: int32 [8, 4], P('clus'), may hold values from 1 to 16, 32 in all within a row
- aggregate: bfloat16 [512, 96], replicated, may hold values from -0.625 to 0.625
- translators: bfloat16 [316, 512], P(None, 'dir'), may hold values from -0.21875 to 0.21875
- boundary_lists: int32 [8, 2, 32], P('clus'), may hold values from 0 to 63
- far_sources: int32 [512, 128], P('clus'), may hold values from 0 to 127
- far_translators: int32 [512, 128], P('clus'), may hold values from 0 to 315
- near_blocks: bfloat16 [512, 96, 576], P(('clus', 'dir')), may hold values from -0.25 to 0.25
- near_columns: int32 [512, 6], P(('clus', 'dir')), may hold values from 0 to 15
Outputs:
- field: bfloat16 [96, 32768], P(None, ('clus', 'dir'))
The draws below stay inside these ranges and needn't reach their ends.
Inputs may be any that keep to these rules, and one draw needn't show every extreme that they name: `live_counts`: A cluster's counts add to 32; in every cluster some device holds all 16 of its slots. `far_sources`: values below 64 name the cluster's own slots, the next 32 the boxes received from the previous cluster, the last 32 those from the next cluster.
All inputs are finite; a program needn't handle non-finite values.
Results may differ from the reference program's by a relative error of at most 0.0075.
Values may be sent and summed in bfloat16 or wider, within the bound.
A program may use at most 64 MiB of HBM per device.

```python
import math
import jax
import jax.numpy as jnp
import numpy as np
from jax import lax

U = 96
K = 512
R = 64
NTR = 316
NI = 128
NN = 6
NBND = 32
BCAP = 16
BOX_CL = 32
S_CL = 64
S_EXT = 128
SLOTS = 512
N_CLUS = 8
N_DIR = 4


def place_ends(entries, key, low, high):
    longest = entries.shape.index(max(entries.shape))
    spots = []
    for shift in (0, 1):
        where = [jax.random.randint(jax.random.fold_in(key, axis), (), 0, length) for axis, length in enumerate(entries.shape)]
        where[longest] = (where[longest] + shift) % entries.shape[longest]
        spots.append(tuple(where))
    return entries.at[spots[0]].set(low).at[spots[1]].set(high)


def level_of(rng, extent, pieces, low, top_value):
    def one(dim, blocks):
        draws = jax.random.uniform(jax.random.fold_in(jax.random.fold_in(rng, 6), dim), (blocks,), jnp.float32, low / len(pieces), top_value / len(pieces))
        return jnp.repeat(jnp.exp(draws), extent[dim] // blocks).reshape((-1,) + (1,) * (len(extent) - dim - 1))

    gain = one(*pieces[0])
    for cut in pieces[1:]:
        gain = gain * one(*cut)
    return gain


def profile(count, total, most, lean):
    portions = [(1 << 20) // math.isqrt(grade ** lean) + 1 for grade in range(2, count + 1)]
    surplus, given = total - most - (count - 1), [1] * (count - 1)
    while surplus > 0:
        free = [i for i in range(count - 1) if given[i] < most]
        mass, remaining = sum([portions[i] for i in free]), surplus
        for i in free:
            addition = min(most - given[i], max(1, remaining * portions[i] // mass), surplus)
            given[i] = given[i] + addition
            surplus = surplus - addition
    return np.array([most] + given)


def ragged_sizes(rng, amount, total, most, skew):
    if amount == 2:
        one = jax.random.randint(rng, (), max(1, total - most), min(most, total - 1) + 1)
        return jnp.stack([one, total - one])
    tallies = jnp.asarray(profile(amount, total, most, skew), jnp.int32)
    twos = (amount - 1) // 2
    donor, sink = tallies[1:1 + 2 * twos:2], tallies[2:2 + 2 * twos:2]
    margin = jnp.minimum(donor - 1, most - sink)
    shifted = jax.random.randint(jax.random.fold_in(rng, 1), (twos,), 0, 1 << 20) % (margin + 1)
    tallies = tallies.at[1:1 + 2 * twos:2].set(donor - shifted).at[2:2 + 2 * twos:2].set(sink + shifted)
    return tallies[jax.random.permutation(jax.random.fold_in(rng, 2), amount)]


def noise(rng, shape, width, limit, split=(), held_as=jnp.bfloat16):
    array = width * jax.random.normal(rng, shape, jnp.float32)
    if split:
        array = array * level_of(rng, shape, split, -0.22, 0.18)
    return jnp.clip(array, -limit, limit).astype(held_as)


def setup_inputs(seed: int = 0) -> dict:
    keys = jax.random.split(jax.random.key(seed), 10)
    return {
        "sources": noise(keys[0], (U, SLOTS * R), 1.0, 6.0, ((1, 32),)),
        "live_counts": jax.vmap(lambda own: ragged_sizes(own, N_DIR, BOX_CL, BCAP, 2))(jax.random.split(keys[1], N_CLUS)).reshape((N_CLUS, N_DIR)).astype(jnp.int32),
        "aggregate": noise(keys[2], (K, U), U ** -0.5, 0.625),
        "translators": noise(keys[3], (NTR, K), (NI * K // U) ** -0.5, 0.21875, ((1, 4),)),
        "boundary_lists": place_ends(jax.random.randint(keys[4], (N_CLUS, 2, NBND), 0, S_CL), jax.random.fold_in(keys[4], 1), 0, S_CL - 1).astype(jnp.int32),
        "far_sources": place_ends(jax.random.randint(keys[5], (SLOTS, NI), 0, S_EXT), jax.random.fold_in(keys[5], 1), 0, S_EXT - 1).astype(jnp.int32),
        "far_translators": place_ends(jax.random.randint(keys[6], (SLOTS, NI), 0, NTR), jax.random.fold_in(keys[6], 1), 0, NTR - 1).astype(jnp.int32),
        "near_blocks": noise(keys[7], (SLOTS, U, NN * U), (NN * U) ** -0.5, 0.25, ((0, 32),)),
        "near_columns": place_ends(jax.random.randint(keys[8], (SLOTS, NN), 0, BCAP), jax.random.fold_in(keys[8], 1), 0, BCAP - 1).astype(jnp.int32),
    }


def reference(sources, live_counts, aggregate, translators, boundary_lists, far_sources, far_translators, near_blocks, near_columns):
    live_mask = (jnp.arange(BCAP, dtype=jnp.int32)[None, None, :] < live_counts[:, :, None]).reshape(SLOTS)
    masked = sources.reshape(U, SLOTS, R) * live_mask.astype(jnp.bfloat16)[None, :, None]
    pattern = jnp.dot(aggregate, masked.reshape(U, SLOTS * R), preferred_element_type=jnp.float32).astype(jnp.bfloat16)
    pattern = pattern.reshape(K, N_CLUS, S_CL, R)
    empty_block = jnp.zeros((K, 1, S_CL, R), jnp.bfloat16)
    padded = jnp.concatenate([empty_block, pattern, empty_block], axis=1)
    empty_list = jnp.zeros((1, 2, NBND), jnp.int32)
    padded_lists = jnp.concatenate([empty_list, boundary_lists, empty_list], axis=0)
    kind_table = translators.astype(jnp.float32)
    target_rows = jnp.broadcast_to(jnp.arange(S_CL, dtype=jnp.int32)[:, None], (S_CL, NI))
    slot_base = (jnp.arange(S_CL, dtype=jnp.int32) // BCAP) * BCAP

    def cluster_field(cluster):
        own_block = lax.dynamic_index_in_dim(padded, cluster + 1, 1, keepdims=False)
        before = lax.dynamic_index_in_dim(padded, cluster, 1, keepdims=False)
        following = lax.dynamic_index_in_dim(padded, cluster + 2, 1, keepdims=False)
        before_list = lax.dynamic_index_in_dim(padded_lists, cluster, 0, keepdims=False)[0]
        following_list = lax.dynamic_index_in_dim(padded_lists, cluster + 2, 0, keepdims=False)[1]
        extended = jnp.concatenate([own_block, before[:, before_list, :], following[:, following_list, :]], axis=1).astype(jnp.float32)
        first_row = cluster * S_CL
        sources_here = lax.dynamic_slice_in_dim(far_sources, first_row, S_CL, 0)
        kinds_here = lax.dynamic_slice_in_dim(far_translators, first_row, S_CL, 0)
        weights = jnp.zeros((S_CL, S_EXT, K), jnp.float32).at[target_rows, sources_here].add(kind_table[kinds_here])
        incoming = jnp.einsum("tsk,ksr->ktr", weights, extended, precision=lax.Precision.HIGHEST).astype(jnp.bfloat16)
        far_part = jnp.dot(aggregate.T, incoming.reshape(K, S_CL * R), preferred_element_type=jnp.float32)
        local_units = lax.dynamic_slice_in_dim(masked, first_row, S_CL, 1)
        neighbour_slots = lax.dynamic_slice_in_dim(near_columns, first_row, S_CL, 0) + slot_base[:, None]
        stacked = local_units[:, neighbour_slots, :].astype(jnp.float32)
        blocks = lax.dynamic_slice_in_dim(near_blocks, first_row, S_CL, 0).astype(jnp.float32).reshape(S_CL, U, NN, U)
        near_part = jnp.einsum("sujv,vsjr->usr", blocks, stacked, precision=lax.Precision.HIGHEST)
        return far_part + near_part.reshape(U, S_CL * R)

    fields = lax.map(cluster_field, jnp.arange(N_CLUS, dtype=jnp.int32))
    summed = fields.transpose(1, 0, 2).reshape(U, SLOTS, R) * live_mask.astype(jnp.float32)[None, :, None]
    return summed.reshape(U, SLOTS * R).astype(jnp.bfloat16)
```

```python
import jax
import jax.numpy as jnp
from jax import lax
from jax.sharding import PartitionSpec as P


def shifted(value, axis, steps):
    count = lax.axis_size(axis)
    leading, last = (max(0, -steps), min(count, count - steps))
    return lax.ppermute(value, axis, [(source, source + steps) for source in range(leading, last)])


def one_hot(ids, count):
    return (ids[..., None] == jnp.arange(count, dtype=jnp.int32)).astype(jnp.bfloat16)


def per_device(
    sources,
    live_counts,
    aggregate,
    translators,
    boundary_lists,
    far_sources,
    far_translators,
    near_blocks,
    near_columns,
):
    dir_index = lax.axis_index("dir")
    unknowns = sources.shape[0]
    directions = aggregate.shape[0]
    capacity = near_blocks.shape[0]
    rights = sources.shape[1] // capacity
    cluster_slots = far_sources.shape[0]
    neighbours = near_columns.shape[1]
    bound_count = boundary_lists.shape[2]
    f32 = jnp.float32
    counts = live_counts[0]
    own_count = lax.dynamic_index_in_dim(counts, dir_index, 0, keepdims=False)
    own_live = jnp.arange(capacity, dtype=jnp.int32) < own_count
    units = sources.reshape(unknowns, capacity, rights) * own_live.astype(jnp.bfloat16)[None, :, None]
    gathered = lax.all_gather(
        units.reshape(unknowns, capacity * rights), "dir", axis=1, tiled=True
    ).reshape(unknowns, cluster_slots, rights)
    kinds = lax.all_gather(translators, "dir", axis=1, tiled=True)
    passed = jnp.einsum(
        "bms,usr->bumr",
        one_hot(boundary_lists[0], cluster_slots),
        gathered,
        preferred_element_type=f32,
    ).astype(jnp.bfloat16)
    up = shifted(passed[0].reshape(unknowns, -1), "clus", 1)
    down = shifted(passed[1].reshape(unknowns, -1), "clus", -1)
    extended = jnp.concatenate([gathered.reshape(unknowns, -1), up, down], axis=1)
    ext_slots = cluster_slots + 2 * bound_count
    pattern = (
        jnp.dot(aggregate, extended, preferred_element_type=f32)
        .astype(jnp.bfloat16)
        .reshape(directions, ext_slots, rights)
    )
    own_sources = lax.dynamic_slice_in_dim(far_sources, dir_index * capacity, capacity, 0)
    own_kinds = lax.dynamic_slice_in_dim(far_translators, dir_index * capacity, capacity, 0)
    values = jnp.einsum(
        "tin,nk->tik",
        one_hot(own_kinds, kinds.shape[0]),
        kinds,
        preferred_element_type=f32,
    ).astype(jnp.bfloat16)
    weights = jnp.einsum(
        "tis,tik->kts", one_hot(own_sources, ext_slots), values, preferred_element_type=f32
    ).astype(jnp.bfloat16)
    incoming = jnp.einsum("kts,ksr->ktr", weights, pattern, preferred_element_type=f32).astype(
        jnp.bfloat16
    )
    far_part = jnp.dot(
        aggregate.T, incoming.reshape(directions, capacity * rights), preferred_element_type=f32
    )
    stacked = jnp.einsum(
        "sjq,uqr->sjur", one_hot(near_columns, capacity), units, preferred_element_type=f32
    ).astype(jnp.bfloat16)
    near_part = jnp.einsum(
        "suv,svr->usr",
        near_blocks,
        stacked.reshape(capacity, neighbours * unknowns, rights),
        preferred_element_type=f32,
    )
    summed = (far_part.reshape(unknowns, capacity, rights) + near_part) * own_live.astype(f32)[
        None, :, None
    ]
    return summed.reshape(unknowns, capacity * rights).astype(jnp.bfloat16)


def solution(mesh):
    in_specs = (
        P(None, ("clus", "dir")),
        P("clus", None),
        P(),
        P(None, "dir"),
        P("clus", None, None),
        P("clus", None),
        P("clus", None),
        P(("clus", "dir"), None, None),
        P(("clus", "dir"), None),
    )
    out_specs = P(None, ("clus", "dir"))
    return jax.shard_map(
        per_device, mesh=mesh, in_specs=in_specs, out_specs=out_specs, check_vma=False
    )
```

```python
import functools

import jax
import jax.numpy as jnp
from jax import lax
from jax.experimental import pallas as pl
from jax.experimental.pallas import tpu as pltpu
from jax.sharding import PartitionSpec as P

LANES = 128
F32 = jnp.float32
BF16 = jnp.bfloat16
VMEM = pltpu.VMEM
SMEM = pltpu.SMEM


def exchange(n_dir, n_clus, pair_ref, half_ref, units_ref, table_ref, all_ref, before_ref, after_ref,
             kinds_ref, up_ref, down_ref, send_sem, recv_sem, tsend_sem, trecv_sem, bsend_sem, brecv_sem):
    me = lax.axis_index("dir")
    cluster = lax.axis_index("clus")
    has_before = cluster > 0
    has_after = cluster < n_clus - 1
    pairs = units_ref.shape[0]
    rows = table_ref.shape[0]
    barrier = pltpu.get_barrier_semaphore()
    for step in range(1, n_dir):
        pl.semaphore_signal(barrier, inc=1, device_id={"dir": lax.rem(me + step, n_dir)},
                            device_id_type=pl.DeviceIdType.MESH)

    @pl.when(has_before)
    def _():
        pl.semaphore_signal(barrier, inc=1, device_id={"clus": cluster - 1},
                            device_id_type=pl.DeviceIdType.MESH)

    @pl.when(has_after)
    def _():
        pl.semaphore_signal(barrier, inc=1, device_id={"clus": cluster + 1},
                            device_id_type=pl.DeviceIdType.MESH)

    sides = has_before.astype(jnp.int32) + has_after.astype(jnp.int32)
    pl.semaphore_wait(barrier, n_dir - 1 + sides)

    own = pl.ds(me * pairs, pairs)
    own_rows = pl.ds(pl.multiple_of(me * rows, rows), rows)
    copies = []
    for src, dst, ss, rs in (
        (units_ref, all_ref.at[own], send_sem, recv_sem),
        (table_ref, kinds_ref.at[own_rows], tsend_sem, trecv_sem),
    ):
        for step in range(1, n_dir):
            copy = pltpu.make_async_remote_copy(
                src_ref=src, dst_ref=dst, send_sem=ss.at[step], recv_sem=rs.at[step],
                device_id={"dir": lax.rem(me + step, n_dir)}, device_id_type=pl.DeviceIdType.MESH)
            copy.start()
            copies.append(copy)
    all_ref[own] = units_ref[...]
    kinds_ref[own_rows] = table_ref[...]

    @pl.when(jnp.logical_not(has_before))
    def _():
        before_ref[...] = jnp.zeros_like(before_ref)

    @pl.when(jnp.logical_not(has_after))
    def _():
        after_ref[...] = jnp.zeros_like(after_ref)

    for copy in copies[: n_dir - 1]:
        copy.wait_recv()
    width = units_ref.shape[2] // 2

    def pick(row, m):
        value = all_ref[pair_ref[row, m]]
        return jnp.where(half_ref[row, m] == 1, value[:, width:], value[:, :width])

    upward = pltpu.make_async_remote_copy(
        src_ref=up_ref, dst_ref=before_ref, send_sem=bsend_sem.at[0], recv_sem=brecv_sem.at[0],
        device_id={"clus": cluster + 1}, device_id_type=pl.DeviceIdType.MESH)
    downward = pltpu.make_async_remote_copy(
        src_ref=down_ref, dst_ref=after_ref, send_sem=bsend_sem.at[1], recv_sem=brecv_sem.at[1],
        device_id={"clus": cluster - 1}, device_id_type=pl.DeviceIdType.MESH)
    for row, (ref, there, copy) in enumerate(
        ((up_ref, has_after, upward), (down_ref, has_before, downward))
    ):
        def fill(p, carry, row=row, ref=ref):
            ref[p] = jnp.concatenate([pick(row, 2 * p), pick(row, 2 * p + 1)], axis=1)
            return carry

        lax.fori_loop(0, ref.shape[0], fill, 0)

        @pl.when(there)
        def _(copy=copy):
            copy.start()

    for copy in copies[n_dir - 1 :]:
        copy.wait_recv()
    for copy in copies:
        copy.wait_send()

    @pl.when(has_after)
    def _():
        upward.wait_send()
        downward.wait_recv()

    @pl.when(has_before)
    def _():
        downward.wait_send()
        upward.wait_recv()


def compute(count_ref, near_cols_ref, all_ref, before_ref, after_ref, kinds_ref, agg_ref, aggt_ref,
            units_ref, src_ids_ref, kind_ids_ref, near_ref, out_ref, e_ref, w_ref, inc_ref, acc_ref, near_acc_ref,
            local_ref, stack_ref):
    step = pl.program_id(0)
    block = agg_ref.shape[0]
    capacity, unknowns, rights = local_ref.shape
    own_pairs, bound_pairs = all_ref.shape[0], before_ref.shape[0]
    pairs = own_pairs + 2 * bound_pairs
    chunk = near_ref.shape[0]
    neighbours = near_cols_ref.shape[1]
    interactions = src_ids_ref.shape[1]

    @pl.when(step == 0)
    def _():
        acc_ref[...] = jnp.zeros_like(acc_ref)
        for s in range(capacity):
            lo = (s % 2) * rights
            local_ref[s] = units_ref[s // 2, :, lo : lo + rights]

    rows = agg_ref[...]

    def patterns(ref, first):
        def body(p, carry):
            two = jnp.concatenate([ref[2 * p], ref[2 * p + 1]], axis=1)
            made = jnp.dot(rows, two, preferred_element_type=F32)
            at = pl.multiple_of((first + 2 * p) * block, block)
            e_ref[pl.ds(at, block), :] = made[:, :LANES]
            e_ref[pl.ds(at + block, block), :] = made[:, LANES:]
            return carry

        lax.fori_loop(0, ref.shape[0] // 2, body, 0, unroll=4)

    patterns(all_ref, 0)
    patterns(before_ref, own_pairs)
    patterns(after_ref, own_pairs + bound_pairs)

    table = kinds_ref[...]
    kind_rows = lax.broadcasted_iota(jnp.int32, (table.shape[1], interactions), 0)
    place = lax.broadcasted_iota(jnp.int32, (2 * pairs, interactions), 0)
    slot_rows = jnp.where(place < pairs, 2 * place, 2 * (place - pairs) + 1)

    def weigh(t, carry):
        pick_kind = jnp.where(kind_rows == kind_ids_ref[pl.ds(t, 1), :], 1.0, 0.0).astype(BF16)
        values = jnp.dot(table, pick_kind, preferred_element_type=F32).astype(BF16)
        pick_source = jnp.where(slot_rows == src_ids_ref[pl.ds(t, 1), :], 1.0, 0.0).astype(BF16)
        made = lax.dot_general(values, pick_source, (((1,), (1,)), ((), ())),
                               preferred_element_type=F32)
        for half in range(2):
            at = pl.multiple_of((half * capacity + t) * block, block)
            for c in range(w_ref.shape[0]):
                lo, hi = c * LANES, min((c + 1) * LANES, pairs)
                w_ref[c, pl.ds(at, block), : hi - lo] = made[:, half * pairs + lo : half * pairs + hi]
        return carry

    lax.fori_loop(0, capacity, weigh, 0, unroll=2)

    def translate(k, carry):
        e = e_ref[pl.ds(k, pairs, stride=block), :].astype(BF16)
        w = [w_ref[c, pl.ds(k, 2 * capacity, stride=block), :] for c in range(w_ref.shape[0])]
        w = jnp.concatenate(w, axis=1)[:, :pairs].astype(BF16)
        o = jnp.dot(w, e, preferred_element_type=F32)
        at = pl.multiple_of(k * capacity, capacity)
        inc_ref[pl.ds(at, capacity), :rights] = o[:capacity, :rights] + o[capacity:, rights:]
        return carry

    lax.fori_loop(0, block, translate, 0, unroll=8)

    columns = aggt_ref[...]
    for p in range(capacity // 2):
        two = [inc_ref[pl.ds(2 * p + h, block, stride=capacity), :][:, :rights] for h in range(2)]
        two = jnp.concatenate(two, axis=1).astype(BF16)
        acc_ref[p] += jnp.dot(columns, two, preferred_element_type=F32)

    for p in range(chunk // 2):
        parts = []
        for h in range(2):
            s = step * chunk + 2 * p + h
            for j in range(neighbours):
                stack_ref[h, j * unknowns : (j + 1) * unknowns, :] = local_ref[near_cols_ref[s, j]]
            parts.append(jnp.dot(near_ref[2 * p + h], stack_ref[h], preferred_element_type=F32))
        near_acc_ref[step * (chunk // 2) + p] = jnp.concatenate(parts, axis=1)

    @pl.when(step == pl.num_programs(0) - 1)
    def _():
        side = lax.broadcasted_iota(jnp.int32, (unknowns, LANES), 1) // rights
        for p in range(capacity // 2):
            total = jnp.where(side + 2 * p < count_ref[0], acc_ref[p] + near_acc_ref[p], 0.0)
            out_ref[:, p * LANES : (p + 1) * LANES] = total.astype(BF16)


def per_device(
    sources,
    live_counts,
    aggregate,
    translators,
    boundary_lists,
    far_sources,
    far_translators,
    near_blocks,
    near_columns,
):
    n_dir, n_clus = lax.axis_size("dir"), lax.axis_size("clus")
    dir_index = lax.axis_index("dir")
    unknowns = sources.shape[0]
    directions = aggregate.shape[0]
    capacity = near_blocks.shape[0]
    rights = sources.shape[1] // capacity
    slots, interactions = far_sources.shape
    neighbours = near_columns.shape[1]
    bound = boundary_lists.shape[2]
    dir_slice = translators.shape[1]
    block = LANES
    steps = directions // block
    chunk = capacity // steps
    pairs = (slots + 2 * bound) // 2
    own_count = lax.dynamic_slice_in_dim(live_counts[0], dir_index, 1, 0)
    live = jnp.arange(capacity, dtype=jnp.int32) < own_count[0]
    units = sources.reshape(unknowns, capacity, rights) * live.astype(BF16)[None, :, None]
    units = units.reshape(unknowns, capacity // 2, 2 * rights).transpose(1, 0, 2)
    kind_width = -(-translators.shape[0] // LANES) * LANES
    table = jnp.pad(translators.T, ((0, 0), (0, kind_width - translators.shape[0])))
    sent = (bound // 2, unknowns, 2 * rights)
    gathered, before, after, kinds = pl.pallas_call(
        functools.partial(exchange, n_dir, n_clus),
        out_shape=[
            jax.ShapeDtypeStruct((slots // 2, unknowns, 2 * rights), BF16),
            jax.ShapeDtypeStruct(sent, BF16),
            jax.ShapeDtypeStruct(sent, BF16),
            jax.ShapeDtypeStruct((directions, kind_width), BF16),
        ],
        in_specs=[pl.BlockSpec(memory_space=SMEM)] * 2 + [pl.BlockSpec(memory_space=VMEM)] * 2,
        out_specs=[pl.BlockSpec(memory_space=VMEM)] * 4,
        scratch_shapes=[VMEM(sent, BF16), VMEM(sent, BF16)]
        + [pltpu.SemaphoreType.DMA((n_dir,))] * 4
        + [pltpu.SemaphoreType.DMA((2,))] * 2,
        compiler_params=pltpu.CompilerParams(
            collective_id=0, has_side_effects=True, vmem_limit_bytes=32 * 2**20
        ),
        name="exchange",
    )(boundary_lists[0] // 2, boundary_lists[0] % 2, units, table)
    own_sources = lax.dynamic_slice_in_dim(far_sources, dir_index * capacity, capacity, 0)
    own_kinds = lax.dynamic_slice_in_dim(far_translators, dir_index * capacity, capacity, 0)

    def whole(shape):
        return pl.BlockSpec(shape, lambda i: (0,) * len(shape))

    return pl.pallas_call(
        compute,
        grid=(steps,),
        out_shape=jax.ShapeDtypeStruct((unknowns, capacity * rights), BF16),
        in_specs=[
            pl.BlockSpec(memory_space=SMEM),
            pl.BlockSpec(memory_space=SMEM),
            whole(gathered.shape),
            whole(before.shape),
            whole(after.shape),
            pl.BlockSpec((block, kind_width), lambda i: (i, 0)),
            pl.BlockSpec((block, unknowns), lambda i: (i, 0)),
            pl.BlockSpec((unknowns, block), lambda i: (0, i)),
            whole(units.shape),
            whole(own_sources.shape),
            whole(own_kinds.shape),
            pl.BlockSpec((chunk, unknowns, neighbours * unknowns), lambda i: (i, 0, 0)),
        ],
        out_specs=whole((unknowns, capacity * rights)),
        scratch_shapes=[
            VMEM((pairs * block, LANES), F32),
            VMEM((-(-pairs // LANES), 2 * capacity * block, LANES), F32),
            VMEM((block * capacity, LANES), F32),
            VMEM((capacity // 2, unknowns, LANES), F32),
            VMEM((capacity // 2, unknowns, LANES), F32),
            VMEM((capacity, unknowns, rights), BF16),
            VMEM((2, neighbours * unknowns, rights), BF16),
        ],
        compiler_params=pltpu.CompilerParams(vmem_limit_bytes=48 * 2**20),
        name="compute",
    )(own_count, near_columns, gathered, before, after, kinds, aggregate, aggregate.T, units,
      own_sources, own_kinds, near_blocks)


def solution(mesh):
    in_specs = (
        P(None, ("clus", "dir")),
        P("clus", None),
        P(),
        P(None, "dir"),
        P("clus", None, None),
        P("clus", None),
        P("clus", None),
        P(("clus", "dir"), None, None),
        P(("clus", "dir"), None),
    )
    out_specs = P(None, ("clus", "dir"))
    return jax.shard_map(
        per_device, mesh=mesh, in_specs=in_specs, out_specs=out_specs, check_vma=False
    )
```

```python
import functools

import jax
import jax.numpy as jnp
from jax import lax
from jax.experimental import pallas as pl
from jax.experimental.pallas import tpu as pltpu
from jax.sharding import PartitionSpec as P

LANES = 128
GAP = 8
SCRATCH_BYTES = 32 * 2**20
F32 = jnp.float32
BF16 = jnp.bfloat16
VMEM = pltpu.VMEM
SMEM = pltpu.SMEM


def exchange(n_dir, n_clus, pair_ref, half_ref, units_ref, table_ref, all_ref, before_ref, after_ref,
             kinds_ref, up_ref, down_ref, send_sem, recv_sem, tsend_sem, trecv_sem, bsend_sem, brecv_sem):
    me = lax.axis_index("dir")
    cluster = lax.axis_index("clus")
    has_before = cluster > 0
    has_after = cluster < n_clus - 1
    pairs = units_ref.shape[0]
    rows = table_ref.shape[0]
    barrier = pltpu.get_barrier_semaphore()
    for step in range(1, n_dir):
        pl.semaphore_signal(barrier, inc=1, device_id={"dir": lax.rem(me + step, n_dir)},
                            device_id_type=pl.DeviceIdType.MESH)

    @pl.when(has_before)
    def _():
        pl.semaphore_signal(barrier, inc=1, device_id={"clus": cluster - 1},
                            device_id_type=pl.DeviceIdType.MESH)

    @pl.when(has_after)
    def _():
        pl.semaphore_signal(barrier, inc=1, device_id={"clus": cluster + 1},
                            device_id_type=pl.DeviceIdType.MESH)

    sides = has_before.astype(jnp.int32) + has_after.astype(jnp.int32)
    pl.semaphore_wait(barrier, n_dir - 1 + sides)

    own = pl.ds(me * pairs, pairs)
    own_rows = pl.ds(pl.multiple_of(me * rows, rows), rows)
    copies = []
    for src, dst, ss, rs in (
        (units_ref, all_ref.at[own], send_sem, recv_sem),
        (table_ref, kinds_ref.at[own_rows], tsend_sem, trecv_sem),
    ):
        for step in range(1, n_dir):
            copy = pltpu.make_async_remote_copy(
                src_ref=src, dst_ref=dst, send_sem=ss.at[step], recv_sem=rs.at[step],
                device_id={"dir": lax.rem(me + step, n_dir)}, device_id_type=pl.DeviceIdType.MESH)
            copy.start()
            copies.append(copy)
    all_ref[own] = units_ref[...]
    kinds_ref[own_rows] = table_ref[...]

    @pl.when(jnp.logical_not(has_before))
    def _():
        before_ref[...] = jnp.zeros_like(before_ref)

    @pl.when(jnp.logical_not(has_after))
    def _():
        after_ref[...] = jnp.zeros_like(after_ref)

    for copy in copies[: n_dir - 1]:
        copy.wait_recv()
    width = units_ref.shape[2] // 2

    def pick(row, m):
        value = all_ref[pair_ref[row, m]]
        return jnp.where(half_ref[row, m] == 1, value[:, width:], value[:, :width])

    upward = pltpu.make_async_remote_copy(
        src_ref=up_ref, dst_ref=before_ref, send_sem=bsend_sem.at[0], recv_sem=brecv_sem.at[0],
        device_id={"clus": cluster + 1}, device_id_type=pl.DeviceIdType.MESH)
    downward = pltpu.make_async_remote_copy(
        src_ref=down_ref, dst_ref=after_ref, send_sem=bsend_sem.at[1], recv_sem=brecv_sem.at[1],
        device_id={"clus": cluster - 1}, device_id_type=pl.DeviceIdType.MESH)
    for row, (ref, there, copy) in enumerate(
        ((up_ref, has_after, upward), (down_ref, has_before, downward))
    ):
        def fill(p, carry, row=row, ref=ref):
            ref[p] = jnp.concatenate([pick(row, 2 * p), pick(row, 2 * p + 1)], axis=1)
            return carry

        lax.fori_loop(0, ref.shape[0], fill, 0)

        @pl.when(there)
        def _(copy=copy):
            copy.start()

    for copy in copies[n_dir - 1 :]:
        copy.wait_recv()
    for copy in copies:
        copy.wait_send()

    @pl.when(has_after)
    def _():
        upward.wait_send()
        downward.wait_recv()

    @pl.when(has_before)
    def _():
        downward.wait_send()
        upward.wait_recv()


def compute(count_ref, near_cols_ref, all_ref, before_ref, after_ref, kinds_ref, agg_ref, aggt_ref,
            units_ref, src_ids_ref, kind_ids_ref, near_ref, out_ref, e_ref, w_ref, inc_ref, acc_ref, near_acc_ref,
            local_ref, stack_ref):
    step = pl.program_id(0)
    block = agg_ref.shape[0]
    stride = block + GAP
    capacity, unknowns, rights = local_ref.shape
    own_pairs, bound_pairs = all_ref.shape[0], before_ref.shape[0]
    pairs = own_pairs + 2 * bound_pairs
    chunk = near_ref.shape[0]
    neighbours = near_cols_ref.shape[1]
    interactions = src_ids_ref.shape[1]

    @pl.when(step == 0)
    def _():
        acc_ref[...] = jnp.zeros_like(acc_ref)
        for s in range(capacity):
            lo = (s % 2) * rights
            local_ref[s] = units_ref[s // 2, :, lo : lo + rights]

    rows = agg_ref[...]

    def patterns(ref, first):
        def body(p, carry):
            two = jnp.concatenate([ref[2 * p], ref[2 * p + 1]], axis=1)
            made = jnp.dot(rows, two, preferred_element_type=F32)
            at = pl.multiple_of((first + 2 * p) * stride, GAP)
            e_ref[pl.ds(at, block), :] = made[:, :LANES]
            e_ref[pl.ds(at + stride, block), :] = made[:, LANES:]
            return carry

        lax.fori_loop(0, ref.shape[0] // 2, body, 0, unroll=8)

    patterns(all_ref, 0)
    patterns(before_ref, own_pairs)
    patterns(after_ref, own_pairs + bound_pairs)

    table = kinds_ref[...]
    kind_rows = lax.broadcasted_iota(jnp.int32, (table.shape[1], interactions), 0)
    place = lax.broadcasted_iota(jnp.int32, (2 * pairs, interactions), 0)
    slot_rows = jnp.where(place < pairs, 2 * place, 2 * (place - pairs) + 1)

    def weigh(t, carry):
        pick_kind = jnp.where(kind_rows == kind_ids_ref[pl.ds(t, 1), :], 1.0, 0.0).astype(BF16)
        values = jnp.dot(table, pick_kind, preferred_element_type=F32).astype(BF16)
        pick_source = jnp.where(slot_rows == src_ids_ref[pl.ds(t, 1), :], 1.0, 0.0).astype(BF16)
        made = lax.dot_general(values, pick_source, (((1,), (1,)), ((), ())),
                               preferred_element_type=F32)
        for half in range(2):
            at = pl.multiple_of((half * capacity + t) * stride, GAP)
            for c in range(w_ref.shape[0]):
                lo, hi = c * LANES, min((c + 1) * LANES, pairs)
                w_ref[c, pl.ds(at, block), : hi - lo] = made[:, half * pairs + lo : half * pairs + hi]
        return carry

    lax.fori_loop(0, capacity, weigh, 0, unroll=8)

    def translate(k, carry):
        e = e_ref[pl.ds(k, pairs, stride=stride), :].astype(BF16)
        w = [w_ref[c, pl.ds(k, 2 * capacity, stride=stride), :] for c in range(w_ref.shape[0])]
        w = jnp.concatenate(w, axis=1)[:, :pairs].astype(BF16)
        o = jnp.dot(w, e, preferred_element_type=F32)
        at = pl.multiple_of(k * capacity, capacity)
        inc_ref[pl.ds(at, capacity), :rights] = o[:capacity, :rights] + o[capacity:, rights:]
        return carry

    lax.fori_loop(0, block, translate, 0, unroll=64)

    columns = aggt_ref[...]
    for p in range(capacity // 2):
        two = [inc_ref[pl.ds(2 * p + h, block, stride=capacity), :][:, :rights] for h in range(2)]
        two = jnp.concatenate(two, axis=1).astype(BF16)
        acc_ref[p] += jnp.dot(columns, two, preferred_element_type=F32)

    for p in range(chunk // 2):
        parts = []
        for h in range(2):
            s = step * chunk + 2 * p + h
            for j in range(neighbours):
                stack_ref[h, j * unknowns : (j + 1) * unknowns, :] = local_ref[near_cols_ref[s, j]]
            parts.append(jnp.dot(near_ref[2 * p + h], stack_ref[h], preferred_element_type=F32))
        near_acc_ref[step * (chunk // 2) + p] = jnp.concatenate(parts, axis=1)

    @pl.when(step == pl.num_programs(0) - 1)
    def _():
        side = lax.broadcasted_iota(jnp.int32, (unknowns, LANES), 1) // rights
        for p in range(capacity // 2):
            total = jnp.where(side + 2 * p < count_ref[0], acc_ref[p] + near_acc_ref[p], 0.0)
            out_ref[:, p * LANES : (p + 1) * LANES] = total.astype(BF16)


def per_device(
    sources,
    live_counts,
    aggregate,
    translators,
    boundary_lists,
    far_sources,
    far_translators,
    near_blocks,
    near_columns,
):
    n_dir, n_clus = lax.axis_size("dir"), lax.axis_size("clus")
    dir_index = lax.axis_index("dir")
    unknowns = sources.shape[0]
    directions = aggregate.shape[0]
    capacity = near_blocks.shape[0]
    rights = sources.shape[1] // capacity
    slots, interactions = far_sources.shape
    neighbours = near_columns.shape[1]
    bound = boundary_lists.shape[2]
    dir_slice = translators.shape[1]
    pairs = (slots + 2 * bound) // 2
    weight_groups = -(-pairs // LANES)
    row_bytes = (pairs + weight_groups * 2 * capacity) * LANES * 4
    block = directions
    while block > LANES and row_bytes * block > SCRATCH_BYTES:
        block //= 2
    steps = directions // block
    chunk = capacity // steps
    own_count = lax.dynamic_slice_in_dim(live_counts[0], dir_index, 1, 0)
    live = jnp.arange(capacity, dtype=jnp.int32) < own_count[0]
    units = sources.reshape(unknowns, capacity, rights) * live.astype(BF16)[None, :, None]
    units = units.reshape(unknowns, capacity // 2, 2 * rights).transpose(1, 0, 2)
    kind_width = -(-translators.shape[0] // LANES) * LANES
    table = jnp.pad(translators.T, ((0, 0), (0, kind_width - translators.shape[0])))
    sent = (bound // 2, unknowns, 2 * rights)
    gathered, before, after, kinds = pl.pallas_call(
        functools.partial(exchange, n_dir, n_clus),
        out_shape=[
            jax.ShapeDtypeStruct((slots // 2, unknowns, 2 * rights), BF16),
            jax.ShapeDtypeStruct(sent, BF16),
            jax.ShapeDtypeStruct(sent, BF16),
            jax.ShapeDtypeStruct((directions, kind_width), BF16),
        ],
        in_specs=[pl.BlockSpec(memory_space=SMEM)] * 2 + [pl.BlockSpec(memory_space=VMEM)] * 2,
        out_specs=[pl.BlockSpec(memory_space=VMEM)] * 4,
        scratch_shapes=[VMEM(sent, BF16), VMEM(sent, BF16)]
        + [pltpu.SemaphoreType.DMA((n_dir,))] * 4
        + [pltpu.SemaphoreType.DMA((2,))] * 2,
        compiler_params=pltpu.CompilerParams(
            collective_id=0, has_side_effects=True, vmem_limit_bytes=32 * 2**20
        ),
        name="exchange",
    )(boundary_lists[0] // 2, boundary_lists[0] % 2, units, table)
    own_sources = lax.dynamic_slice_in_dim(far_sources, dir_index * capacity, capacity, 0)
    own_kinds = lax.dynamic_slice_in_dim(far_translators, dir_index * capacity, capacity, 0)

    def whole(shape):
        return pl.BlockSpec(shape, lambda i: (0,) * len(shape))

    return pl.pallas_call(
        compute,
        grid=(steps,),
        out_shape=jax.ShapeDtypeStruct((unknowns, capacity * rights), BF16),
        in_specs=[
            pl.BlockSpec(memory_space=SMEM),
            pl.BlockSpec(memory_space=SMEM),
            whole(gathered.shape),
            whole(before.shape),
            whole(after.shape),
            pl.BlockSpec((block, kind_width), lambda i: (i, 0)),
            pl.BlockSpec((block, unknowns), lambda i: (i, 0)),
            pl.BlockSpec((unknowns, block), lambda i: (0, i)),
            whole(units.shape),
            whole(own_sources.shape),
            whole(own_kinds.shape),
            pl.BlockSpec((chunk, unknowns, neighbours * unknowns), lambda i: (i, 0, 0)),
        ],
        out_specs=whole((unknowns, capacity * rights)),
        scratch_shapes=[
            VMEM((pairs * (block + GAP), LANES), F32),
            VMEM((weight_groups, 2 * capacity * (block + GAP), LANES), F32),
            VMEM((block * capacity, LANES), F32),
            VMEM((capacity // 2, unknowns, LANES), F32),
            VMEM((capacity // 2, unknowns, LANES), F32),
            VMEM((capacity, unknowns, rights), BF16),
            VMEM((2, neighbours * unknowns, rights), BF16),
        ],
        compiler_params=pltpu.CompilerParams(vmem_limit_bytes=56 * 2**20),
        name="compute",
    )(own_count, near_columns, gathered, before, after, kinds, aggregate, aggregate.T, units,
      own_sources, own_kinds, near_blocks)


def solution(mesh):
    in_specs = (
        P(None, ("clus", "dir")),
        P("clus", None),
        P(),
        P(None, "dir"),
        P("clus", None, None),
        P("clus", None),
        P("clus", None),
        P(("clus", "dir"), None, None),
        P(("clus", "dir"), None),
    )
    out_specs = P(None, ("clus", "dir"))
    return jax.shard_map(
        per_device, mesh=mesh, in_specs=in_specs, out_specs=out_specs, check_vma=False
    )
```

```python
import functools

import jax
import jax.numpy as jnp
from jax import lax
from jax.experimental import pallas as pl
from jax.experimental.pallas import tpu as pltpu
from jax.sharding import PartitionSpec as P

LANES = 128
CHUNKS = 2
GAP = 8
SCRATCH_BYTES = 32 * 2**20
F32 = jnp.float32
BF16 = jnp.bfloat16
VMEM = pltpu.VMEM
SMEM = pltpu.SMEM


def exchange(n_dir, n_clus, pair_ref, half_ref, units_ref, table_ref, all_ref, before_ref, after_ref,
             kinds_ref, up_ref, down_ref, send_sem, recv_sem, tsend_sem, trecv_sem, bsend_sem, brecv_sem):
    me = lax.axis_index("dir")
    cluster = lax.axis_index("clus")
    has_before = cluster > 0
    has_after = cluster < n_clus - 1
    pairs = units_ref.shape[0]
    rows = table_ref.shape[0]
    barrier = pltpu.get_barrier_semaphore()
    for step in range(1, n_dir):
        pl.semaphore_signal(barrier, inc=1, device_id={"dir": lax.rem(me + step, n_dir)},
                            device_id_type=pl.DeviceIdType.MESH)

    @pl.when(has_before)
    def _():
        pl.semaphore_signal(barrier, inc=1, device_id={"clus": cluster - 1},
                            device_id_type=pl.DeviceIdType.MESH)

    @pl.when(has_after)
    def _():
        pl.semaphore_signal(barrier, inc=1, device_id={"clus": cluster + 1},
                            device_id_type=pl.DeviceIdType.MESH)

    sides = has_before.astype(jnp.int32) + has_after.astype(jnp.int32)
    pl.semaphore_wait(barrier, n_dir - 1 + sides)

    own = pl.ds(me * pairs, pairs)
    own_rows = pl.ds(pl.multiple_of(me * rows, rows), rows)
    all_ref[own] = units_ref[...]
    kinds_ref[own_rows] = table_ref[...]
    part = pairs // CHUNKS

    def hop(side, distance, chunk):
        sign = 1 - 2 * side
        owner = me - sign * (distance - 1)
        target = me + sign
        came = me - sign * distance
        sends = (owner >= 0) & (owner < n_dir) & (target >= 0) & (target < n_dir)
        where = all_ref.at[pl.ds(owner * pairs + chunk * part, part)]
        copy = pltpu.make_async_remote_copy(
            src_ref=where, dst_ref=where, send_sem=send_sem.at[side, distance, chunk],
            recv_sem=recv_sem.at[side, distance, chunk],
            device_id={"dir": target}, device_id_type=pl.DeviceIdType.MESH)
        there = all_ref.at[pl.ds(came * pairs + chunk * part, part)]
        arrival = pltpu.make_async_remote_copy(
            src_ref=there, dst_ref=there, send_sem=send_sem.at[side, distance, chunk],
            recv_sem=recv_sem.at[side, distance, chunk],
            device_id={"dir": target}, device_id_type=pl.DeviceIdType.MESH)
        return copy, sends, arrival, (came >= 0) & (came < n_dir)

    def launch(distance, side, chunk):
        @pl.when(hop(side, distance, chunk)[1])
        def _():
            hop(side, distance, chunk)[0].start()

    lanes_of = [(chunk, side) for chunk in range(CHUNKS) for side in range(2)]
    for chunk, side in lanes_of:
        launch(1, side, chunk)
    @pl.when(jnp.logical_not(has_before))
    def _():
        before_ref[...] = jnp.zeros_like(before_ref)

    @pl.when(jnp.logical_not(has_after))
    def _():
        after_ref[...] = jnp.zeros_like(after_ref)

    for distance in range(1, n_dir):
        for chunk, side in lanes_of:
            @pl.when(hop(side, distance, chunk)[3])
            def _(side=side, distance=distance, chunk=chunk):
                hop(side, distance, chunk)[2].wait_recv()

            if distance < n_dir - 1:
                launch(distance + 1, side, chunk)

    core = lax.rem(cluster, 2)
    half = rows // 2
    tables, relays = [], []
    for step in range(1, n_dir):
        mine = kinds_ref.at[pl.ds(pl.multiple_of(me * rows + core * half, half), half)]
        tables.append(pltpu.make_async_remote_copy(
            src_ref=mine, dst_ref=mine, send_sem=tsend_sem.at[0, step], recv_sem=trecv_sem.at[0, step],
            device_id={"dir": lax.rem(me + step, n_dir)}, device_id_type=pl.DeviceIdType.MESH))
        owner = lax.rem(me + n_dir - step, n_dir)
        got = kinds_ref.at[pl.ds(pl.multiple_of(owner * rows + core * half, half), half)]
        relays.append(pltpu.make_async_remote_copy(
            src_ref=got, dst_ref=got, send_sem=tsend_sem.at[1, step], recv_sem=trecv_sem.at[1, step],
            device_id={"clus": cluster + 1 - 2 * core}, device_id_type=pl.DeviceIdType.MESH))
    for copy in tables:
        copy.start()
    width = units_ref.shape[2] // 2

    def pick(row, m):
        value = all_ref[pair_ref[row, m]]
        return jnp.where(half_ref[row, m] == 1, value[:, width:], value[:, :width])

    upward = pltpu.make_async_remote_copy(
        src_ref=up_ref, dst_ref=before_ref, send_sem=bsend_sem.at[0], recv_sem=brecv_sem.at[0],
        device_id={"clus": cluster + 1}, device_id_type=pl.DeviceIdType.MESH)
    downward = pltpu.make_async_remote_copy(
        src_ref=down_ref, dst_ref=after_ref, send_sem=bsend_sem.at[1], recv_sem=brecv_sem.at[1],
        device_id={"clus": cluster - 1}, device_id_type=pl.DeviceIdType.MESH)
    for row, (ref, there, copy) in enumerate(
        ((up_ref, has_after, upward), (down_ref, has_before, downward))
    ):
        def fill(p, carry, row=row, ref=ref):
            ref[p] = jnp.concatenate([pick(row, 2 * p), pick(row, 2 * p + 1)], axis=1)
            return carry

        lax.fori_loop(0, ref.shape[0], fill, 0)

        @pl.when(there)
        def _(copy=copy):
            copy.start()

    for copy, relay in zip(tables, relays):
        copy.wait_recv()
        relay.start()
    for copy in relays:
        copy.wait_recv()
    for copy in tables + relays:
        copy.wait_send()
    for distance in range(1, n_dir):
        for chunk, side in lanes_of:
            @pl.when(hop(side, distance, chunk)[1])
            def _(side=side, distance=distance, chunk=chunk):
                hop(side, distance, chunk)[0].wait_send()

    @pl.when(has_after)
    def _():
        upward.wait_send()
        downward.wait_recv()

    @pl.when(has_before)
    def _():
        downward.wait_send()
        upward.wait_recv()


def compute(count_ref, near_cols_ref, all_ref, before_ref, after_ref, kinds_ref, agg_ref, aggt_ref,
            units_ref, src_ids_ref, kind_ids_ref, near_ref, out_ref, e_ref, w_ref, inc_ref, acc_ref, near_acc_ref,
            local_ref, stack_ref):
    step = pl.program_id(0)
    block = agg_ref.shape[0]
    stride = block + GAP
    capacity, unknowns, rights = local_ref.shape
    own_pairs, bound_pairs = all_ref.shape[0], before_ref.shape[0]
    pairs = own_pairs + 2 * bound_pairs
    chunk = near_ref.shape[0]
    neighbours = near_cols_ref.shape[1]
    interactions = src_ids_ref.shape[1]

    @pl.when(step == 0)
    def _():
        acc_ref[...] = jnp.zeros_like(acc_ref)
        for s in range(capacity):
            lo = (s % 2) * rights
            local_ref[s] = units_ref[s // 2, :, lo : lo + rights]

    rows = agg_ref[...]

    def patterns(ref, first):
        def body(p, carry):
            two = jnp.concatenate([ref[2 * p], ref[2 * p + 1]], axis=1)
            made = jnp.dot(rows, two, preferred_element_type=F32)
            at = pl.multiple_of((first + 2 * p) * stride, GAP)
            e_ref[pl.ds(at, block), :] = made[:, :LANES]
            e_ref[pl.ds(at + stride, block), :] = made[:, LANES:]
            return carry

        lax.fori_loop(0, ref.shape[0] // 2, body, 0, unroll=8)

    patterns(all_ref, 0)
    patterns(before_ref, own_pairs)
    patterns(after_ref, own_pairs + bound_pairs)

    table = kinds_ref[...]
    kind_rows = lax.broadcasted_iota(jnp.int32, (table.shape[1], interactions), 0)
    place = lax.broadcasted_iota(jnp.int32, (2 * pairs, interactions), 0)
    slot_rows = jnp.where(place < pairs, 2 * place, 2 * (place - pairs) + 1)

    def weigh(t, carry):
        pick_kind = jnp.where(kind_rows == kind_ids_ref[pl.ds(t, 1), :], 1.0, 0.0).astype(BF16)
        values = jnp.dot(table, pick_kind, preferred_element_type=F32).astype(BF16)
        pick_source = jnp.where(slot_rows == src_ids_ref[pl.ds(t, 1), :], 1.0, 0.0).astype(BF16)
        made = lax.dot_general(values, pick_source, (((1,), (1,)), ((), ())),
                               preferred_element_type=F32)
        for half in range(2):
            at = pl.multiple_of((half * capacity + t) * stride, GAP)
            for c in range(w_ref.shape[0]):
                lo, hi = c * LANES, min((c + 1) * LANES, pairs)
                w_ref[c, pl.ds(at, block), : hi - lo] = made[:, half * pairs + lo : half * pairs + hi]
        return carry

    lax.fori_loop(0, capacity, weigh, 0, unroll=8)

    def translate(k, carry):
        e = e_ref[pl.ds(k, pairs, stride=stride), :].astype(BF16)
        w = [w_ref[c, pl.ds(k, 2 * capacity, stride=stride), :] for c in range(w_ref.shape[0])]
        w = jnp.concatenate(w, axis=1)[:, :pairs].astype(BF16)
        o = jnp.dot(w, e, preferred_element_type=F32)
        at = pl.multiple_of(k * capacity, capacity)
        inc_ref[pl.ds(at, capacity), :rights] = o[:capacity, :rights] + o[capacity:, rights:]
        return carry

    lax.fori_loop(0, block, translate, 0, unroll=64)

    columns = aggt_ref[...]
    for p in range(capacity // 2):
        two = [inc_ref[pl.ds(2 * p + h, block, stride=capacity), :][:, :rights] for h in range(2)]
        two = jnp.concatenate(two, axis=1).astype(BF16)
        acc_ref[p] += jnp.dot(columns, two, preferred_element_type=F32)

    for p in range(chunk // 2):
        parts = []
        for h in range(2):
            s = step * chunk + 2 * p + h
            for j in range(neighbours):
                stack_ref[h, j * unknowns : (j + 1) * unknowns, :] = local_ref[near_cols_ref[s, j]]
            parts.append(jnp.dot(near_ref[2 * p + h], stack_ref[h], preferred_element_type=F32))
        near_acc_ref[step * (chunk // 2) + p] = jnp.concatenate(parts, axis=1)

    @pl.when(step == pl.num_programs(0) - 1)
    def _():
        side = lax.broadcasted_iota(jnp.int32, (unknowns, LANES), 1) // rights
        for p in range(capacity // 2):
            total = jnp.where(side + 2 * p < count_ref[0], acc_ref[p] + near_acc_ref[p], 0.0)
            out_ref[:, p * LANES : (p + 1) * LANES] = total.astype(BF16)


def per_device(
    sources,
    live_counts,
    aggregate,
    translators,
    boundary_lists,
    far_sources,
    far_translators,
    near_blocks,
    near_columns,
):
    n_dir, n_clus = lax.axis_size("dir"), lax.axis_size("clus")
    dir_index = lax.axis_index("dir")
    unknowns = sources.shape[0]
    directions = aggregate.shape[0]
    capacity = near_blocks.shape[0]
    rights = sources.shape[1] // capacity
    slots, interactions = far_sources.shape
    neighbours = near_columns.shape[1]
    bound = boundary_lists.shape[2]
    dir_slice = translators.shape[1]
    pairs = (slots + 2 * bound) // 2
    weight_groups = -(-pairs // LANES)
    row_bytes = (pairs + weight_groups * 2 * capacity) * LANES * 4
    block = directions
    while block > LANES and row_bytes * block > SCRATCH_BYTES:
        block //= 2
    steps = directions // block
    chunk = capacity // steps
    own_count = lax.dynamic_slice_in_dim(live_counts[0], dir_index, 1, 0)
    live = jnp.arange(capacity, dtype=jnp.int32) < own_count[0]
    units = sources.reshape(unknowns, capacity, rights) * live.astype(BF16)[None, :, None]
    units = units.reshape(unknowns, capacity // 2, 2 * rights).transpose(1, 0, 2)
    kind_width = -(-translators.shape[0] // LANES) * LANES
    table = jnp.pad(translators.T, ((0, 0), (0, kind_width - translators.shape[0])))
    sent = (bound // 2, unknowns, 2 * rights)
    gathered, before, after, kinds = pl.pallas_call(
        functools.partial(exchange, n_dir, n_clus),
        out_shape=[
            jax.ShapeDtypeStruct((slots // 2, unknowns, 2 * rights), BF16),
            jax.ShapeDtypeStruct(sent, BF16),
            jax.ShapeDtypeStruct(sent, BF16),
            jax.ShapeDtypeStruct((directions, kind_width), BF16),
        ],
        in_specs=[pl.BlockSpec(memory_space=SMEM)] * 2 + [pl.BlockSpec(memory_space=VMEM)] * 2,
        out_specs=[pl.BlockSpec(memory_space=VMEM)] * 4,
        scratch_shapes=[VMEM(sent, BF16), VMEM(sent, BF16)]
        + [pltpu.SemaphoreType.DMA((2, n_dir, CHUNKS))] * 2
        + [pltpu.SemaphoreType.DMA((2, n_dir))] * 2
        + [pltpu.SemaphoreType.DMA((2,))] * 2,
        compiler_params=pltpu.CompilerParams(
            collective_id=0, has_side_effects=True, vmem_limit_bytes=32 * 2**20
        ),
        name="exchange",
    )(boundary_lists[0] // 2, boundary_lists[0] % 2, units, table)
    own_sources = lax.dynamic_slice_in_dim(far_sources, dir_index * capacity, capacity, 0)
    own_kinds = lax.dynamic_slice_in_dim(far_translators, dir_index * capacity, capacity, 0)

    def whole(shape):
        return pl.BlockSpec(shape, lambda i: (0,) * len(shape))

    return pl.pallas_call(
        compute,
        grid=(steps,),
        out_shape=jax.ShapeDtypeStruct((unknowns, capacity * rights), BF16),
        in_specs=[
            pl.BlockSpec(memory_space=SMEM),
            pl.BlockSpec(memory_space=SMEM),
            whole(gathered.shape),
            whole(before.shape),
            whole(after.shape),
            pl.BlockSpec((block, kind_width), lambda i: (i, 0)),
            pl.BlockSpec((block, unknowns), lambda i: (i, 0)),
            pl.BlockSpec((unknowns, block), lambda i: (0, i)),
            whole(units.shape),
            whole(own_sources.shape),
            whole(own_kinds.shape),
            pl.BlockSpec((chunk, unknowns, neighbours * unknowns), lambda i: (i, 0, 0)),
        ],
        out_specs=whole((unknowns, capacity * rights)),
        scratch_shapes=[
            VMEM((pairs * (block + GAP), LANES), F32),
            VMEM((weight_groups, 2 * capacity * (block + GAP), LANES), F32),
            VMEM((block * capacity, LANES), F32),
            VMEM((capacity // 2, unknowns, LANES), F32),
            VMEM((capacity // 2, unknowns, LANES), F32),
            VMEM((capacity, unknowns, rights), BF16),
            VMEM((2, neighbours * unknowns, rights), BF16),
        ],
        compiler_params=pltpu.CompilerParams(vmem_limit_bytes=56 * 2**20),
        name="compute",
    )(own_count, near_columns, gathered, before, after, kinds, aggregate, aggregate.T, units,
      own_sources, own_kinds, near_blocks)


def solution(mesh):
    in_specs = (
        P(None, ("clus", "dir")),
        P("clus", None),
        P(),
        P(None, "dir"),
        P("clus", None, None),
        P("clus", None),
        P("clus", None),
        P(("clus", "dir"), None, None),
        P(("clus", "dir"), None),
    )
    out_specs = P(None, ("clus", "dir"))
    return jax.shard_map(
        per_device, mesh=mesh, in_specs=in_specs, out_specs=out_specs, check_vma=False
    )
```

```python
import functools

import jax
import jax.numpy as jnp
from jax import lax
from jax.experimental import pallas as pl
from jax.experimental.pallas import tpu as pltpu
from jax.sharding import PartitionSpec as P

LANES = 128
CHUNKS = 4
GAP = 8
SCRATCH_BYTES = 32 * 2**20
F32 = jnp.float32
BF16 = jnp.bfloat16
VMEM = pltpu.VMEM
SMEM = pltpu.SMEM


def exchange(n_dir, n_clus, pair_ref, half_ref, units_ref, table_ref, all_ref, before_ref, after_ref,
             kinds_ref, up_ref, down_ref, send_sem, recv_sem, tsend_sem, trecv_sem, bsend_sem, brecv_sem):
    me = lax.axis_index("dir")
    cluster = lax.axis_index("clus")
    has_before = cluster > 0
    has_after = cluster < n_clus - 1
    pairs = units_ref.shape[0]
    rows = table_ref.shape[0]
    barrier = pltpu.get_barrier_semaphore()
    for step in range(1, n_dir):
        pl.semaphore_signal(barrier, inc=1, device_id={"dir": lax.rem(me + step, n_dir)},
                            device_id_type=pl.DeviceIdType.MESH)

    @pl.when(has_before)
    def _():
        pl.semaphore_signal(barrier, inc=1, device_id={"clus": cluster - 1},
                            device_id_type=pl.DeviceIdType.MESH)

    @pl.when(has_after)
    def _():
        pl.semaphore_signal(barrier, inc=1, device_id={"clus": cluster + 1},
                            device_id_type=pl.DeviceIdType.MESH)

    sides = has_before.astype(jnp.int32) + has_after.astype(jnp.int32)
    pl.semaphore_wait(barrier, n_dir - 1 + sides)

    own = pl.ds(me * pairs, pairs)
    own_rows = pl.ds(pl.multiple_of(me * rows, rows), rows)
    all_ref[own] = units_ref[...]
    kinds_ref[own_rows] = table_ref[...]
    part = pairs // CHUNKS

    def hop(side, distance, chunk):
        sign = 1 - 2 * side
        owner = me - sign * (distance - 1)
        target = me + sign
        came = me - sign * distance
        sends = (owner >= 0) & (owner < n_dir) & (target >= 0) & (target < n_dir)
        where = all_ref.at[pl.ds(owner * pairs + chunk * part, part)]
        copy = pltpu.make_async_remote_copy(
            src_ref=where, dst_ref=where, send_sem=send_sem.at[side, distance, chunk],
            recv_sem=recv_sem.at[side, distance, chunk],
            device_id={"dir": target}, device_id_type=pl.DeviceIdType.MESH)
        there = all_ref.at[pl.ds(came * pairs + chunk * part, part)]
        arrival = pltpu.make_async_remote_copy(
            src_ref=there, dst_ref=there, send_sem=send_sem.at[side, distance, chunk],
            recv_sem=recv_sem.at[side, distance, chunk],
            device_id={"dir": target}, device_id_type=pl.DeviceIdType.MESH)
        return copy, sends, arrival, (came >= 0) & (came < n_dir)

    def launch(distance, side, chunk):
        @pl.when(hop(side, distance, chunk)[1])
        def _():
            hop(side, distance, chunk)[0].start()

    lanes_of = [(chunk, side) for chunk in range(CHUNKS) for side in range(2)]
    for chunk, side in lanes_of:
        launch(1, side, chunk)
    @pl.when(jnp.logical_not(has_before))
    def _():
        before_ref[...] = jnp.zeros_like(before_ref)

    @pl.when(jnp.logical_not(has_after))
    def _():
        after_ref[...] = jnp.zeros_like(after_ref)

    for distance in range(1, n_dir):
        for chunk, side in lanes_of:
            @pl.when(hop(side, distance, chunk)[3])
            def _(side=side, distance=distance, chunk=chunk):
                hop(side, distance, chunk)[2].wait_recv()

            if distance < n_dir - 1:
                launch(distance + 1, side, chunk)

    core = lax.rem(cluster, 2)
    half = rows // 2
    tables, relays = [], []
    for step in range(1, n_dir):
        mine = kinds_ref.at[pl.ds(pl.multiple_of(me * rows + core * half, half), half)]
        tables.append(pltpu.make_async_remote_copy(
            src_ref=mine, dst_ref=mine, send_sem=tsend_sem.at[0, step], recv_sem=trecv_sem.at[0, step],
            device_id={"dir": lax.rem(me + step, n_dir)}, device_id_type=pl.DeviceIdType.MESH))
        owner = lax.rem(me + n_dir - step, n_dir)
        got = kinds_ref.at[pl.ds(pl.multiple_of(owner * rows + core * half, half), half)]
        relays.append(pltpu.make_async_remote_copy(
            src_ref=got, dst_ref=got, send_sem=tsend_sem.at[1, step], recv_sem=trecv_sem.at[1, step],
            device_id={"clus": cluster + 1 - 2 * core}, device_id_type=pl.DeviceIdType.MESH))
    for copy in tables:
        copy.start()
    width = units_ref.shape[2] // 2

    def pick(row, m):
        value = all_ref[pair_ref[row, m]]
        return jnp.where(half_ref[row, m] == 1, value[:, width:], value[:, :width])

    upward = pltpu.make_async_remote_copy(
        src_ref=up_ref, dst_ref=before_ref, send_sem=bsend_sem.at[0], recv_sem=brecv_sem.at[0],
        device_id={"clus": cluster + 1}, device_id_type=pl.DeviceIdType.MESH)
    downward = pltpu.make_async_remote_copy(
        src_ref=down_ref, dst_ref=after_ref, send_sem=bsend_sem.at[1], recv_sem=brecv_sem.at[1],
        device_id={"clus": cluster - 1}, device_id_type=pl.DeviceIdType.MESH)
    for row, (ref, there, copy) in enumerate(
        ((up_ref, has_after, upward), (down_ref, has_before, downward))
    ):
        def fill(p, carry, row=row, ref=ref):
            ref[p] = jnp.concatenate([pick(row, 2 * p), pick(row, 2 * p + 1)], axis=1)
            return carry

        lax.fori_loop(0, ref.shape[0], fill, 0, unroll=4)

        @pl.when(there)
        def _(copy=copy):
            copy.start()

    for copy, relay in zip(tables, relays):
        copy.wait_recv()
        relay.start()
    for copy in relays:
        copy.wait_recv()
    for copy in tables + relays:
        copy.wait_send()
    for distance in range(1, n_dir):
        for chunk, side in lanes_of:
            @pl.when(hop(side, distance, chunk)[1])
            def _(side=side, distance=distance, chunk=chunk):
                hop(side, distance, chunk)[0].wait_send()

    @pl.when(has_after)
    def _():
        upward.wait_send()
        downward.wait_recv()

    @pl.when(has_before)
    def _():
        downward.wait_send()
        upward.wait_recv()


def compute(count_ref, near_cols_ref, all_ref, before_ref, after_ref, kinds_ref, agg_ref, aggt_ref,
            units_ref, src_ids_ref, kind_ids_ref, near_ref, out_ref, e_ref, w_ref, inc_ref, acc_ref, near_acc_ref,
            local_ref, stack_ref):
    step = pl.program_id(0)
    block = agg_ref.shape[0]
    stride = block + GAP
    capacity, unknowns, rights = local_ref.shape
    own_pairs, bound_pairs = all_ref.shape[0], before_ref.shape[0]
    pairs = own_pairs + 2 * bound_pairs
    chunk = near_ref.shape[0]
    neighbours = near_cols_ref.shape[1]
    interactions = src_ids_ref.shape[1]

    @pl.when(step == 0)
    def _():
        acc_ref[...] = jnp.zeros_like(acc_ref)
        for s in range(capacity):
            lo = (s % 2) * rights
            local_ref[s] = units_ref[s // 2, :, lo : lo + rights]

    rows = agg_ref[...]

    def patterns(ref, first):
        def body(p, carry):
            two = jnp.concatenate([ref[2 * p], ref[2 * p + 1]], axis=1)
            made = jnp.dot(rows, two, preferred_element_type=F32)
            at = pl.multiple_of((first + 2 * p) * stride, GAP)
            e_ref[pl.ds(at, block), :] = made[:, :LANES]
            e_ref[pl.ds(at + stride, block), :] = made[:, LANES:]
            return carry

        lax.fori_loop(0, ref.shape[0] // 2, body, 0, unroll=8)

    patterns(all_ref, 0)
    patterns(before_ref, own_pairs)
    patterns(after_ref, own_pairs + bound_pairs)

    table = kinds_ref[...]
    kind_rows = lax.broadcasted_iota(jnp.int32, (table.shape[1], interactions), 0)
    place = lax.broadcasted_iota(jnp.int32, (2 * pairs, interactions), 0)
    slot_rows = jnp.where(place < pairs, 2 * place, 2 * (place - pairs) + 1)

    def weigh(t, carry):
        pick_kind = jnp.where(kind_rows == kind_ids_ref[pl.ds(t, 1), :], 1.0, 0.0).astype(BF16)
        values = jnp.dot(table, pick_kind, preferred_element_type=F32).astype(BF16)
        pick_source = jnp.where(slot_rows == src_ids_ref[pl.ds(t, 1), :], 1.0, 0.0).astype(BF16)
        made = lax.dot_general(values, pick_source, (((1,), (1,)), ((), ())),
                               preferred_element_type=F32)
        for half in range(2):
            at = pl.multiple_of((half * capacity + t) * stride, GAP)
            for c in range(w_ref.shape[0]):
                lo, hi = c * LANES, min((c + 1) * LANES, pairs)
                w_ref[c, pl.ds(at, block), : hi - lo] = made[:, half * pairs + lo : half * pairs + hi]
        return carry

    lax.fori_loop(0, capacity, weigh, 0, unroll=16)

    def translate(k, carry):
        e = e_ref[pl.ds(k, pairs, stride=stride), :].astype(BF16)
        w = [w_ref[c, pl.ds(k, 2 * capacity, stride=stride), :] for c in range(w_ref.shape[0])]
        w = jnp.concatenate(w, axis=1)[:, :pairs].astype(BF16)
        o = jnp.dot(w, e, preferred_element_type=F32)
        at = pl.multiple_of(k * capacity, capacity)
        inc_ref[pl.ds(at, capacity), :rights] = o[:capacity, :rights] + o[capacity:, rights:]
        return carry

    lax.fori_loop(0, block, translate, 0, unroll=64)

    columns = aggt_ref[...]
    for p in range(capacity // 2):
        two = [inc_ref[pl.ds(2 * p + h, block, stride=capacity), :][:, :rights] for h in range(2)]
        two = jnp.concatenate(two, axis=1).astype(BF16)
        acc_ref[p] += jnp.dot(columns, two, preferred_element_type=F32)

    for p in range(chunk // 2):
        parts = []
        for h in range(2):
            s = step * chunk + 2 * p + h
            for j in range(neighbours):
                stack_ref[h, j * unknowns : (j + 1) * unknowns, :] = local_ref[near_cols_ref[s, j]]
            parts.append(jnp.dot(near_ref[2 * p + h], stack_ref[h], preferred_element_type=F32))
        near_acc_ref[step * (chunk // 2) + p] = jnp.concatenate(parts, axis=1)

    @pl.when(step == pl.num_programs(0) - 1)
    def _():
        side = lax.broadcasted_iota(jnp.int32, (unknowns, LANES), 1) // rights
        for p in range(capacity // 2):
            total = jnp.where(side + 2 * p < count_ref[0], acc_ref[p] + near_acc_ref[p], 0.0)
            out_ref[:, p * LANES : (p + 1) * LANES] = total.astype(BF16)


def per_device(
    sources,
    live_counts,
    aggregate,
    translators,
    boundary_lists,
    far_sources,
    far_translators,
    near_blocks,
    near_columns,
):
    n_dir, n_clus = lax.axis_size("dir"), lax.axis_size("clus")
    dir_index = lax.axis_index("dir")
    unknowns = sources.shape[0]
    directions = aggregate.shape[0]
    capacity = near_blocks.shape[0]
    rights = sources.shape[1] // capacity
    slots, interactions = far_sources.shape
    neighbours = near_columns.shape[1]
    bound = boundary_lists.shape[2]
    dir_slice = translators.shape[1]
    pairs = (slots + 2 * bound) // 2
    weight_groups = -(-pairs // LANES)
    row_bytes = (pairs + weight_groups * 2 * capacity) * LANES * 4
    block = directions
    while block > LANES and row_bytes * block > SCRATCH_BYTES:
        block //= 2
    steps = directions // block
    chunk = capacity // steps
    own_count = lax.dynamic_slice_in_dim(live_counts[0], dir_index, 1, 0)
    live = jnp.arange(capacity, dtype=jnp.int32) < own_count[0]
    units = sources.reshape(unknowns, capacity, rights) * live.astype(BF16)[None, :, None]
    units = units.reshape(unknowns, capacity // 2, 2 * rights).transpose(1, 0, 2)
    kind_width = -(-translators.shape[0] // LANES) * LANES
    table = jnp.pad(translators.T, ((0, 0), (0, kind_width - translators.shape[0])))
    sent = (bound // 2, unknowns, 2 * rights)
    gathered, before, after, kinds = pl.pallas_call(
        functools.partial(exchange, n_dir, n_clus),
        out_shape=[
            jax.ShapeDtypeStruct((slots // 2, unknowns, 2 * rights), BF16),
            jax.ShapeDtypeStruct(sent, BF16),
            jax.ShapeDtypeStruct(sent, BF16),
            jax.ShapeDtypeStruct((directions, kind_width), BF16),
        ],
        in_specs=[pl.BlockSpec(memory_space=SMEM)] * 2 + [pl.BlockSpec(memory_space=VMEM)] * 2,
        out_specs=[pl.BlockSpec(memory_space=VMEM)] * 4,
        scratch_shapes=[VMEM(sent, BF16), VMEM(sent, BF16)]
        + [pltpu.SemaphoreType.DMA((2, n_dir, CHUNKS))] * 2
        + [pltpu.SemaphoreType.DMA((2, n_dir))] * 2
        + [pltpu.SemaphoreType.DMA((2,))] * 2,
        compiler_params=pltpu.CompilerParams(
            collective_id=0, has_side_effects=True, vmem_limit_bytes=32 * 2**20
        ),
        name="exchange",
    )(boundary_lists[0] // 2, boundary_lists[0] % 2, units, table)
    own_sources = lax.dynamic_slice_in_dim(far_sources, dir_index * capacity, capacity, 0)
    own_kinds = lax.dynamic_slice_in_dim(far_translators, dir_index * capacity, capacity, 0)

    def whole(shape):
        return pl.BlockSpec(shape, lambda i: (0,) * len(shape))

    return pl.pallas_call(
        compute,
        grid=(steps,),
        out_shape=jax.ShapeDtypeStruct((unknowns, capacity * rights), BF16),
        in_specs=[
            pl.BlockSpec(memory_space=SMEM),
            pl.BlockSpec(memory_space=SMEM),
            whole(gathered.shape),
            whole(before.shape),
            whole(after.shape),
            pl.BlockSpec((block, kind_width), lambda i: (i, 0)),
            pl.BlockSpec((block, unknowns), lambda i: (i, 0)),
            pl.BlockSpec((unknowns, block), lambda i: (0, i)),
            whole(units.shape),
            whole(own_sources.shape),
            whole(own_kinds.shape),
            pl.BlockSpec((chunk, unknowns, neighbours * unknowns), lambda i: (i, 0, 0)),
        ],
        out_specs=whole((unknowns, capacity * rights)),
        scratch_shapes=[
            VMEM((pairs * (block + GAP), LANES), F32),
            VMEM((weight_groups, 2 * capacity * (block + GAP), LANES), F32),
            VMEM((block * capacity, LANES), F32),
            VMEM((capacity // 2, unknowns, LANES), F32),
            VMEM((capacity // 2, unknowns, LANES), F32),
            VMEM((capacity, unknowns, rights), BF16),
            VMEM((2, neighbours * unknowns, rights), BF16),
        ],
        compiler_params=pltpu.CompilerParams(vmem_limit_bytes=56 * 2**20),
        name="compute",
    )(own_count, near_columns, gathered, before, after, kinds, aggregate, aggregate.T, units,
      own_sources, own_kinds, near_blocks)


def solution(mesh):
    in_specs = (
        P(None, ("clus", "dir")),
        P("clus", None),
        P(),
        P(None, "dir"),
        P("clus", None, None),
        P("clus", None),
        P("clus", None),
        P(("clus", "dir"), None, None),
        P(("clus", "dir"), None),
    )
    out_specs = P(None, ("clus", "dir"))
    return jax.shard_map(
        per_device, mesh=mesh, in_specs=in_specs, out_specs=out_specs, check_vma=False
    )
```
